256 devices in a mesh: prow: 8 (over x, core), pcol: 32 (over z, y).
Axes of the slice: x: 4, y: 4, z: 8, core: 2. Of those that a mesh axis runs over, the one named last changes fastest.
Arguments:
- b_leaf: bfloat16 [256, 256, 256], P('pcol', 'prow'), may hold values from -6 to 6
- dinv_leaf: bfloat16 [256, 256, 256], P('pcol'), as said below
- b_sep: bfloat16 [64, 256, 256], P('prow', 'pcol'), may hold values from -6 to 6
- dinv_sep: bfloat16 [64, 256, 256], P('prow'), as said below
- coupling: bfloat16 [64, 256, 256, 256], P('prow', 'pcol'), may hold values from -0.03125 to 0.03125
- pattern: int32 [64, 256], P('prow', 'pcol'), may hold values 0 or 1
Outputs:
- x_leaf: float32 [256, 256, 256], P('pcol', 'prow')
- x_sep: float32 [64, 256, 256], P('prow', 'pcol')
The draws below stay inside these ranges and needn't reach their ends.
Inputs may be any that keep to these rules, and one draw needn't show every extreme that they name: pattern holds only 0 and 1. dinv_leaf is a full matrix for every supernode. dinv_sep is a full matrix for every supernode.
All inputs are finite; a program needn't handle non-finite values. No bound on the sum of `pattern` on one device may be relied on, other than what follows from the above.
Results may differ from the reference program's by a relative error of at most 0.0048.
Values may be sent and summed in bfloat16 or wider, within the bound.
No kernel may reach another device: no remote copies, remote signals or barrier semaphores. Data moves between devices by JAX's collectives and lax.ppermute only.
A program may use at most 64 MiB of HBM per device.

```python
import math
import jax
import jax.numpy as jnp
from jax import lax

BS = 256
R = 256
NL = 256
NS = 64


def dominant_blocks(key, count):
    first, second = jax.random.split(key)
    diagonal = jax.random.uniform(first, (count, BS), jnp.float32, 0.6, 1.6)
    noise = jax.random.normal(second, (count, BS, BS), jnp.float32) * (0.5 / math.sqrt(BS))
    eye_block = jnp.eye(BS, dtype=jnp.float32)
    return (eye_block[None, :, :] * diagonal[:, :, None] + noise).astype(jnp.bfloat16)


def draw_dinv_leaf(key, part):
    return dominant_blocks(jax.random.fold_in(key, 11), NL)


def draw_dinv_sep(key, part):
    return dominant_blocks(jax.random.fold_in(key, 23), NS)


def touch_ends(values, own_key, smallest, high):
    longest = values.shape.index(max(values.shape))
    spots = []
    for shift in (0, 1):
        where = [jax.random.randint(jax.random.fold_in(own_key, axis), (), 0, length) for axis, length in enumerate(values.shape)]
        where[longest] = (where[longest] + shift) % values.shape[longest]
        spots.append(tuple(where))
    return values.at[spots[0]].set(smallest).at[spots[1]].set(high)


def shard_levels(rng, shape, cuts, smallest, top_value):
    def one(dim, shards_of):
        heights = jax.random.uniform(jax.random.fold_in(jax.random.fold_in(rng, 6), dim), (shards_of,), jnp.float32, smallest / len(cuts), top_value / len(cuts))
        return jnp.repeat(jnp.exp(heights), shape[dim] // shards_of).reshape((-1,) + (1,) * (len(shape) - dim - 1))

    level = one(*cuts[0])
    for cut in cuts[1:]:
        level = level * one(*cut)
    return level


def centred(own_key, extent, scale, reach, pieces=(), kind=jnp.bfloat16):
    drawn = jax.random.normal(own_key, extent, jnp.float32) * scale
    if len(pieces) > 0:
        drawn = shard_levels(own_key, extent, pieces, -0.22, 0.18) * drawn
    return jnp.clip(drawn, min=-reach, max=reach).astype(kind)


def setup_inputs(seed: int = 0) -> dict:
    seeds = jax.random.split(jax.random.key(seed), 7)
    b_leaf = centred(seeds[0], (NL, R, BS), 1.0, 6.0, ((0, 32), (1, 8)))
    dinv_leaf = draw_dinv_leaf(jax.random.fold_in(seeds[6], 71), 0)
    b_sep = centred(seeds[2], (NS, R, BS), 1.0, 6.0, ((0, 8), (1, 32)))
    dinv_sep = draw_dinv_sep(jax.random.fold_in(seeds[6], 71), 0)
    coupling = centred(seeds[4], (NS, NL, BS, BS), (BS * NL // 2) ** -0.5, 0.03125, ((0, 8), (1, 32)))
    pattern = touch_ends((jax.random.randint(seeds[5], (NS, NL), 0, 2) < 1).astype(jnp.int32), jax.random.fold_in(seeds[5], 1), 0, 1)
    return {"b_leaf": b_leaf, "dinv_leaf": dinv_leaf, "b_sep": b_sep, "dinv_sep": dinv_sep, "coupling": coupling, "pattern": pattern}


def reference(b_leaf, dinv_leaf, b_sep, dinv_sep, coupling, pattern):
    f32 = jnp.float32
    solved = jnp.einsum("lrk,ljk->lrj", b_leaf.astype(f32), dinv_leaf.astype(f32)).astype(jnp.bfloat16)
    solved = lax.optimization_barrier(solved)
    solved_f = solved.astype(f32)

    def forward(item):
        block, mask_row = item
        masked = block.astype(f32) * mask_row.astype(f32)[:, None, None]
        return jnp.einsum("lrk,ljk->rj", solved_f, masked)

    update = lax.map(forward, (coupling, pattern))
    reduced = b_sep.astype(f32) - update
    reduced_b = lax.optimization_barrier(reduced.astype(jnp.bfloat16))
    forward_sep = jnp.einsum("srk,sjk->srj", reduced_b.astype(f32), dinv_sep.astype(f32)).astype(jnp.bfloat16)
    forward_sep = lax.optimization_barrier(forward_sep)
    x_sep = jnp.einsum("srk,skj->srj", forward_sep.astype(f32), dinv_sep.astype(f32))
    x_sep_b = lax.optimization_barrier(x_sep.astype(jnp.bfloat16))

    def backward(carry, item):
        block, mask_row, row_values = item
        masked = block.astype(f32) * mask_row.astype(f32)[:, None, None]
        return carry + jnp.einsum("rj,ljk->lrk", row_values.astype(f32), masked), None

    start = jnp.zeros(solved.shape, f32)
    total, _ = lax.scan(backward, start, (coupling, pattern, x_sep_b))
    corrected = solved_f - total
    corrected_b = lax.optimization_barrier(corrected.astype(jnp.bfloat16))
    x_leaf = jnp.einsum("lrk,lkj->lrj", corrected_b.astype(f32), dinv_leaf.astype(f32))
    return x_leaf, x_sep
```

```python
import jax
import jax.numpy as jnp
from jax import lax
from jax.sharding import Mesh, PartitionSpec as P

BF16 = jnp.bfloat16
F32 = jnp.float32


def separator_values(reduced, dinv_sep):
    reduced_b = reduced.astype(BF16)
    forward_sep = jnp.einsum(
        "srk,sjk->srj", reduced_b, dinv_sep, preferred_element_type=F32
    ).astype(BF16)
    return jnp.einsum("srk,skj->srj", forward_sep, dinv_sep, preferred_element_type=F32)


def swap_core(values):
    return lax.ppermute(values, "core", [(0, 1), (1, 0)])


def gather(values, axis, size):
    copies = jnp.broadcast_to(values[None], (size,) + values.shape)
    return lax.all_to_all(copies, axis, 0, 0, tiled=True)


def shards(b_leaf, dinv_leaf, b_sep, dinv_sep, coupling, pattern):
    core = lax.axis_index("core")
    masked = coupling * pattern.astype(coupling.dtype)[:, :, None, None]
    same_core = lax.all_gather(b_leaf, "x", axis=0, tiled=False)
    other_core = swap_core(same_core)
    first = jnp.where(core == 0, same_core, other_core)
    second = jnp.where(core == 0, other_core, same_core)
    right = jnp.stack([first, second], axis=1)
    solved = jnp.einsum(
        "xclrk,ljk->lxcrj", right, dinv_leaf, preferred_element_type=F32
    ).astype(BF16)
    solved = solved.reshape(8, 256, 256)
    sums = jnp.einsum("lrk,sljk->rsj", solved, masked, preferred_element_type=F32)
    sums = sums.astype(BF16).reshape(32, 8, 8, 256)
    sums = lax.all_to_all(sums, ("z", "y"), 0, 0, tiled=True)
    update = jnp.sum(sums.astype(F32), axis=0)
    reduced = b_sep.astype(F32) - jnp.transpose(update, (1, 0, 2))
    x_sep = separator_values(reduced, dinv_sep)
    x_send = gather(x_sep.astype(BF16), "z", 8)
    x_send = gather(x_send, "y", 4)
    back = jnp.einsum("yzsrj,sljk->zyrlk", x_send, masked, preferred_element_type=F32)
    back = back.reshape(4, 2, 32, 8, 256)
    own = lax.dynamic_index_in_dim(back, core, 1, keepdims=False)
    other = lax.dynamic_index_in_dim(back, 1 - core, 1, keepdims=False)
    pair = own + swap_core(other.astype(BF16)).astype(F32)
    parts = lax.all_to_all(pair.astype(BF16), "x", 0, 0, tiled=True)
    total = jnp.transpose(jnp.sum(parts.astype(F32), axis=0), (1, 0, 2))
    solved_share = jnp.einsum(
        "lrk,ljk->lrj", b_leaf, dinv_leaf, preferred_element_type=F32
    ).astype(BF16)
    corrected = solved_share.astype(F32) - total
    x_leaf = jnp.einsum(
        "lrk,lkj->lrj", corrected.astype(BF16), dinv_leaf, preferred_element_type=F32
    )
    return (x_leaf, x_sep)


def solution(mesh):
    prow, pcol = ("x", "core"), ("z", "y")
    chips = Mesh(mesh.devices.reshape(4, 2, 8, 4), prow + pcol)
    return jax.shard_map(
        shards,
        mesh=chips,
        in_specs=(
            P(pcol, prow, None),
            P(pcol, None, None),
            P(prow, pcol, None),
            P(prow, None, None),
            P(prow, pcol, None, None),
            P(prow, pcol),
        ),
        out_specs=(P(pcol, prow, None), P(prow, pcol, None)),
        check_vma=False,
    )
```

```python
import jax
import jax.numpy as jnp
from jax import lax
from jax.experimental import pallas as pl
from jax.experimental.pallas import tpu as pltpu
from jax.sharding import Mesh, PartitionSpec as P

BF16 = jnp.bfloat16
F32 = jnp.float32
SMEM = pl.BlockSpec(memory_space=pltpu.SMEM)
VMEM = pl.BlockSpec(memory_space=pltpu.VMEM)
HBM = pl.BlockSpec(memory_space=pl.ANY)


def forward_kernel(pattern, solved, stored, far, up, down, own, coupling, sems):
    def fetch(s):
        return pltpu.make_async_copy(stored.at[s], coupling.at[s], sems.at[s])

    for s in range(8):
        fetch(s).start()

    def pair(s2, carry):
        halves = []
        for h in range(2):
            s = 2 * s2 + h
            fetch(s).wait()
            total = None
            for l in range(8):
                left = solved[l] * pattern[s, l].astype(F32).astype(BF16)
                term = lax.dot_general(
                    left, coupling[s, l], (((1,), (1,)), ((), ())), preferred_element_type=F32
                )
                total = term if total is None else total + term
            halves.append(total.reshape(4, 8, 8, 256))
        both = jnp.concatenate(halves, axis=2)
        own[:, s2] = both[0]
        up[:, s2] = both[1]
        far[:, s2] = both[2].astype(BF16)
        down[:, s2] = both[3]
        return carry

    lax.fori_loop(0, 4, pair, 0, unroll=True)


def forward(pattern, solved, coupling):
    def piece(kind):
        return jax.ShapeDtypeStruct((8, 4, 16, 256), kind)

    return pl.pallas_call(
        forward_kernel,
        out_shape=(piece(BF16), piece(F32), piece(F32), piece(F32)),
        in_specs=[SMEM, VMEM, HBM],
        out_specs=(VMEM,) * 4,
        scratch_shapes=[pltpu.VMEM((8, 8, 256, 256), BF16), pltpu.SemaphoreType.DMA((8,))],
        compiler_params=pltpu.CompilerParams(vmem_limit_bytes=48 << 20),
        cost_estimate=pl.CostEstimate(flops=2 << 30, bytes_accessed=11 << 20, transcendentals=0),
        name="forward_sums",
    )(pattern, solved, coupling)


def backward_kernel(pattern, x0, x1, x2, x3, stored, own, send, left, coupling, sems):
    def fetch(l):
        return pltpu.make_async_copy(stored.at[:, l], coupling.at[:, l], sems.at[l])

    for l in range(8):
        fetch(l).start()

    for s2 in range(4):
        for d, x in enumerate((x0, x1, x2, x3)):
            both = x[:, s2].astype(F32).reshape(8, 2, 8, 256)
            for h in range(2):
                left[2 * s2 + h, 64 * d : 64 * d + 64] = both[:, h].reshape(64, 256).astype(BF16)

    def leaf(l, carry):
        fetch(l).wait()
        total = None
        for s in range(8):
            rows = left[s] * pattern[s, l].astype(F32).astype(BF16)
            term = jnp.dot(rows, coupling[s, l], preferred_element_type=F32)
            total = term if total is None else total + term
        parts = total.reshape(4, 4, 2, 8, 256)
        for d in range(0, 4, 2):
            both = jnp.concatenate([parts[d], parts[d + 1]], axis=2)
            own[:, l, 8 * d : 8 * d + 16] = both[:, 0]
            send[:, l, 8 * d : 8 * d + 16] = both[:, 1].astype(BF16)
        return carry

    lax.fori_loop(0, 8, leaf, 0, unroll=4)


def backward(pattern, values, coupling):
    def piece(kind):
        return jax.ShapeDtypeStruct((4, 8, 32, 256), kind)

    return pl.pallas_call(
        backward_kernel,
        out_shape=(piece(F32), piece(BF16)),
        in_specs=[SMEM] + [VMEM] * 4 + [HBM],
        out_specs=(VMEM,) * 2,
        scratch_shapes=[
            pltpu.VMEM((8, 256, 256), BF16),
            pltpu.VMEM((8, 8, 256, 256), BF16),
            pltpu.SemaphoreType.DMA((8,)),
        ],
        compiler_params=pltpu.CompilerParams(vmem_limit_bytes=48 << 20),
        cost_estimate=pl.CostEstimate(flops=2 << 30, bytes_accessed=11 << 20, transcendentals=0),
        name="backward_sums",
    )(pattern, *values, coupling)


def separator_values(reduced, dinv_sep):
    reduced_b = reduced.astype(BF16)
    forward_sep = jnp.einsum(
        "srk,sjk->srj", reduced_b, dinv_sep, preferred_element_type=F32
    ).astype(BF16)
    return jnp.einsum("srk,skj->srj", forward_sep, dinv_sep, preferred_element_type=F32)


def swap_core(values):
    return lax.ppermute(values, "core", [(0, 1), (1, 0)])


def send_on(values, axis):
    return lax.ppermute(values, axis, [(i, (i + 1) % 4) for i in range(4)])


def send_back(values, axis):
    return lax.ppermute(values, axis, [(i, (i + 3) % 4) for i in range(4)])


def send_split(values, axis):
    if axis == "x":
        place, axes = (lambda c, i: 2 * (i % 4) + c), ("x", "core")
    else:
        place, axes = (lambda c, i: 4 * c + i % 4), ("core", "y")
    steps = [(place(0, i), place(0, i + 1)) for i in range(4)]
    steps += [(place(1, i), place(1, i + 3)) for i in range(4)]
    return lax.ppermute(values, axes, steps)


def reduce_axis(own, up, down, far_sent, core, axis):
    far = far_sent.astype(F32)
    up = up + jnp.where(core == 0, far, 0.0)
    down = down + jnp.where(core == 0, 0.0, far)
    up, down = send_on(up.astype(BF16), axis), send_back(down.astype(BF16), axis)
    return own + up.astype(F32) + down.astype(F32)


def gather_axis(own, core, axis):
    up, down = send_back(own, axis), send_on(own, axis)
    far = send_split(jnp.where(core == 0, down, up), axis)
    return own, up, far, down


def shards(b_leaf, dinv_leaf, b_sep, dinv_sep, coupling, pattern):
    x, core, y = lax.axis_index("x"), lax.axis_index("core"), lax.axis_index("y")
    own = jnp.roll(b_leaf.reshape(8, 4, 8, 256), -y, axis=1)
    blocks = gather_axis(own, core, "x")
    near = swap_core(jnp.stack([blocks[0], blocks[1], blocks[3]]))
    far = swap_core(blocks[2])
    right = [blocks[0], near[0], blocks[1], near[1], blocks[2], far, blocks[3], near[2]]
    right = jnp.stack(right, axis=2).reshape(8, 256, 256)
    solved = jnp.einsum(
        "lrk,ljk->lrj", right, dinv_leaf, preferred_element_type=F32
    ).astype(BF16)
    far, up, down, mine = forward(pattern, solved, coupling)
    mine = reduce_axis(mine, up, down, send_split(far, "y"), core, "y")
    mine = mine.astype(BF16).reshape(4, 2, 4, 16, 256)
    mine = jnp.roll(jnp.roll(mine, x, axis=0), core, axis=1).reshape(8, 4, 16, 256)
    sums = lax.all_to_all(mine, "z", 0, 0, tiled=True)
    update = jnp.sum(sums.astype(F32), axis=0).reshape(8, 8, 256)
    x_sep = separator_values(b_sep.astype(F32) - update, dinv_sep)
    copies = jnp.broadcast_to(x_sep.astype(BF16).reshape(1, 4, 16, 256), (8, 4, 16, 256))
    values = lax.all_to_all(copies, "z", 0, 0, tiled=True).reshape(4, 2, 4, 16, 256)
    values = jnp.roll(jnp.roll(values, -x, axis=0), core, axis=1).reshape(8, 4, 16, 256)
    values = gather_axis(values, core, "y")
    kept, sent = backward(pattern, values, coupling)
    pair = kept + swap_core(sent).astype(F32)
    far = send_split(pair[2].astype(BF16), "x")
    total = reduce_axis(pair[0], pair[1], pair[3], far, core, "x")
    solved_share = jnp.einsum(
        "lrk,ljk->lrj", own.reshape(8, 32, 256), dinv_leaf, preferred_element_type=F32
    ).astype(BF16)
    corrected = (solved_share.astype(F32) - total).astype(BF16).reshape(8, 4, 8, 256)
    corrected = jnp.roll(corrected, y, axis=1).reshape(8, 32, 256)
    x_leaf = jnp.einsum("lrk,lkj->lrj", corrected, dinv_leaf, preferred_element_type=F32)
    return (x_leaf, x_sep)


def solution(mesh):
    prow, pcol = ("x", "core"), ("z", "y")
    chips = Mesh(mesh.devices.reshape(4, 2, 8, 4), prow + pcol)
    return jax.shard_map(
        shards,
        mesh=chips,
        in_specs=(
            P(pcol, prow, None),
            P(pcol, None, None),
            P(prow, pcol, None),
            P(prow, None, None),
            P(prow, pcol, None, None),
            P(prow, pcol),
        ),
        out_specs=(P(pcol, prow, None), P(prow, pcol, None)),
        check_vma=False,
    )
```

```python
import jax
import jax.numpy as jnp
from jax import lax
from jax.experimental import pallas as pl
from jax.experimental.pallas import tpu as pltpu
from jax.sharding import Mesh, PartitionSpec as P

BF16 = jnp.bfloat16
F32 = jnp.float32
SMEM = pl.BlockSpec(memory_space=pltpu.SMEM)
VMEM = pl.BlockSpec(memory_space=pltpu.VMEM)


def forward_kernel(pattern, solved, coupling, out):
    for s2 in range(4):
        halves = []
        for s in (2 * s2, 2 * s2 + 1):
            total = None
            for l in range(8):
                left = solved[l] * pattern[s, l].astype(F32).astype(BF16)
                term = lax.dot_general(
                    left, coupling[s, l], (((1,), (1,)), ((), ())), preferred_element_type=F32
                )
                total = term if total is None else total + term
            halves.append(total.reshape(4, 8, 8, 256))
        out[:, :, s2] = jnp.concatenate(halves, axis=2).astype(BF16)


def forward(pattern, solved, coupling):
    return pl.pallas_call(
        forward_kernel,
        out_shape=jax.ShapeDtypeStruct((4, 8, 4, 16, 256), BF16),
        in_specs=[SMEM, VMEM, VMEM],
        out_specs=VMEM,
        compiler_params=pltpu.CompilerParams(vmem_limit_bytes=16 << 20),
        cost_estimate=pl.CostEstimate(flops=2 << 30, bytes_accessed=11 << 20, transcendentals=0),
        name="forward_sums",
    )(pattern, solved, coupling)


def backward_kernel(pattern, values, coupling, kept, sent, left):
    core = lax.axis_index("core")
    for s2 in range(4):
        both = values[:, :, s2].astype(F32)
        for h in range(2):
            rows = both[:, :, 8 * h : 8 * h + 8].reshape(256, 256)
            left[2 * s2 + h] = rows.astype(BF16)
    for l in range(8):
        total = None
        for s in range(8):
            rows = left[s] * pattern[s, l].astype(F32).astype(BF16)
            term = jnp.dot(rows, coupling[s, l], preferred_element_type=F32)
            total = term if total is None else total + term
        parts = total.reshape(4, 4, 2, 8, 256)
        for y in range(0, 4, 2):
            both = jnp.concatenate([parts[y], parts[y + 1]], axis=2)
            kept[:, l, 8 * y : 8 * y + 16] = jnp.where(core == 0, both[:, 0], both[:, 1])
            sent[:, l, 8 * y : 8 * y + 16] = jnp.where(core == 0, both[:, 1], both[:, 0]).astype(BF16)


def backward(pattern, values, coupling):
    def piece(kind):
        return jax.ShapeDtypeStruct((4, 8, 32, 256), kind)

    return pl.pallas_call(
        backward_kernel,
        out_shape=(piece(F32), piece(BF16)),
        in_specs=[SMEM, VMEM, VMEM],
        out_specs=(VMEM,) * 2,
        scratch_shapes=[
            pltpu.VMEM((8, 256, 256), BF16),
        ],
        compiler_params=pltpu.CompilerParams(vmem_limit_bytes=16 << 20),
        cost_estimate=pl.CostEstimate(flops=2 << 30, bytes_accessed=11 << 20, transcendentals=0),
        name="backward_sums",
    )(pattern, values, coupling)


def small(body, out_shape, inputs, name):
    return pl.pallas_call(
        body,
        out_shape=out_shape,
        in_specs=[VMEM] * len(inputs),
        out_specs=jax.tree.map(lambda _: VMEM, out_shape),
        compiler_params=pltpu.CompilerParams(vmem_limit_bytes=16 << 20),
        cost_estimate=pl.CostEstimate(flops=1 << 28, bytes_accessed=2 << 20, transcendentals=0),
        name=name,
    )(*inputs)


def add_kernel(parts, out):
    for z in range(8):
        total = parts[0, z].astype(F32)
        for y in range(1, 4):
            total = total + parts[y, z].astype(F32)
        out[z] = total.astype(BF16)


def separator_kernel(parts, b_sep, dinv, x_sep, copies):
    for s2 in range(4):
        update = parts[0, s2].astype(F32)
        for z in range(1, 8):
            update = update + parts[z, s2].astype(F32)
        values = []
        for h in range(2):
            s = 2 * s2 + h
            reduced = b_sep[s].astype(F32) - update[8 * h : 8 * h + 8]
            forward_sep = lax.dot_general(
                reduced.astype(BF16), dinv[s], (((1,), (1,)), ((), ())), preferred_element_type=F32
            ).astype(BF16)
            value = jnp.dot(forward_sep, dinv[s], preferred_element_type=F32)
            x_sep[s] = value
            values.append(value)
        both = jnp.concatenate(values, axis=0).astype(BF16)
        for z in range(8):
            copies[z, s2] = both


def swap_core(values):
    return lax.ppermute(values, "core", [(0, 1), (1, 0)])


def exchange(values, axis):
    return lax.all_to_all(values, axis, 0, 0, tiled=True)


def shards(b_leaf, dinv_leaf, b_sep, dinv_sep, coupling, pattern):
    shape = jax.ShapeDtypeStruct
    same_core = lax.all_gather(b_leaf, "x", axis=0, tiled=False)
    core = lax.axis_index("core")
    other_core = swap_core(same_core)
    first = jnp.where(core == 0, same_core, other_core)
    second = jnp.where(core == 0, other_core, same_core)
    right = jnp.stack([first, second], axis=1).reshape(8, 8, 4, 8, 256)
    right = jnp.transpose(right, (1, 2, 0, 3, 4)).reshape(8, 256, 256)
    solved = jnp.einsum(
        "lrk,ljk->lrj", right, dinv_leaf, preferred_element_type=F32
    ).astype(BF16)
    sums = exchange(forward(pattern, solved, coupling), "y")
    sums = exchange(small(add_kernel, shape((8, 4, 16, 256), BF16), (sums,), "add_sums"), "z")
    x_sep, copies = small(
        separator_kernel,
        (shape((8, 8, 256), F32), shape((8, 4, 16, 256), BF16)),
        (sums, b_sep, dinv_sep),
        "solve_separators",
    )
    values = exchange(copies, "z")
    values = exchange(jnp.broadcast_to(values[None], (4,) + values.shape), "y")
    kept, sent = backward(pattern, values, coupling)
    pair = kept + swap_core(sent).astype(F32)
    total = jnp.sum(exchange(pair.astype(BF16), "x").astype(F32), axis=0)
    solved_share = jnp.einsum(
        "lrk,ljk->lrj", b_leaf, dinv_leaf, preferred_element_type=F32
    ).astype(BF16)
    corrected = (solved_share.astype(F32) - total).astype(BF16)
    x_leaf = jnp.einsum("lrk,lkj->lrj", corrected, dinv_leaf, preferred_element_type=F32)
    return (x_leaf, x_sep)


def solution(mesh):
    prow, pcol = ("x", "core"), ("z", "y")
    chips = Mesh(mesh.devices.reshape(4, 2, 8, 4), prow + pcol)
    return jax.shard_map(
        shards,
        mesh=chips,
        in_specs=(
            P(pcol, prow, None),
            P(pcol, None, None),
            P(prow, pcol, None),
            P(prow, None, None),
            P(prow, pcol, None, None),
            P(prow, pcol),
        ),
        out_specs=(P(pcol, prow, None), P(prow, pcol, None)),
        check_vma=False,
    )
```

```python
import jax
import jax.numpy as jnp
from jax import lax
from jax.experimental import pallas as pl
from jax.experimental.pallas import tpu as pltpu
from jax.sharding import Mesh, PartitionSpec as P

BF16 = jnp.bfloat16
F32 = jnp.float32
SMEM = pl.BlockSpec(memory_space=pltpu.SMEM)
VMEM = pl.BlockSpec(memory_space=pltpu.VMEM)


def forward_kernel(pattern, solved, coupling, out):
    for s2 in range(4):
        halves = []
        for s in (2 * s2, 2 * s2 + 1):
            total = None
            for l in range(8):
                left = solved[l] * pattern[s, l].astype(F32).astype(BF16)
                term = lax.dot_general(
                    left, coupling[s, l], (((1,), (1,)), ((), ())), preferred_element_type=F32
                )
                total = term if total is None else total + term
            halves.append(total.reshape(8, 4, 8, 256))
        out[:, :, s2] = jnp.concatenate(halves, axis=2).astype(BF16)


def forward(pattern, solved, coupling):
    return pl.pallas_call(
        forward_kernel,
        out_shape=jax.ShapeDtypeStruct((8, 4, 4, 16, 256), BF16),
        in_specs=[SMEM, VMEM, VMEM],
        out_specs=VMEM,
        compiler_params=pltpu.CompilerParams(vmem_limit_bytes=16 << 20),
        cost_estimate=pl.CostEstimate(flops=2 << 30, bytes_accessed=11 << 20, transcendentals=0),
        name="forward_sums",
    )(pattern, solved, coupling)


def backward_kernel(pattern, values, coupling, kept, sent, left):
    core = lax.axis_index("core")
    for s2 in range(4):
        both = values[:, :, s2].astype(F32)
        for h in range(2):
            rows = both[:, :, 8 * h : 8 * h + 8].reshape(256, 256)
            left[2 * s2 + h] = rows.astype(BF16)
    for l in range(8):
        total = None
        for s in range(8):
            rows = left[s] * pattern[s, l].astype(F32).astype(BF16)
            term = jnp.dot(rows, coupling[s, l], preferred_element_type=F32)
            total = term if total is None else total + term
        parts = total.reshape(2, 4, 4, 8, 256)
        for y in range(0, 4, 2):
            both = jnp.concatenate([parts[:, y], parts[:, y + 1]], axis=2)
            kept[:, l, 8 * y : 8 * y + 16] = jnp.where(core == 0, both[0], both[1])
            sent[:, l, 8 * y : 8 * y + 16] = jnp.where(core == 0, both[1], both[0]).astype(BF16)


def backward(pattern, values, coupling):
    def piece(kind):
        return jax.ShapeDtypeStruct((4, 8, 32, 256), kind)

    return pl.pallas_call(
        backward_kernel,
        out_shape=(piece(F32), piece(BF16)),
        in_specs=[SMEM, VMEM, VMEM],
        out_specs=(VMEM,) * 2,
        scratch_shapes=[
            pltpu.VMEM((8, 256, 256), BF16),
        ],
        compiler_params=pltpu.CompilerParams(vmem_limit_bytes=16 << 20),
        cost_estimate=pl.CostEstimate(flops=2 << 30, bytes_accessed=11 << 20, transcendentals=0),
        name="backward_sums",
    )(pattern, values, coupling)


def small(body, out_shape, inputs, name):
    return pl.pallas_call(
        body,
        out_shape=out_shape,
        in_specs=[VMEM] * len(inputs),
        out_specs=jax.tree.map(lambda _: VMEM, out_shape),
        compiler_params=pltpu.CompilerParams(vmem_limit_bytes=16 << 20),
        cost_estimate=pl.CostEstimate(flops=1 << 28, bytes_accessed=2 << 20, transcendentals=0),
        name=name,
    )(*inputs)


def add_kernel(parts, out):
    for z in range(4):
        total = parts[0, z].astype(F32)
        for source in range(1, 8):
            total = total + parts[source, z].astype(F32)
        out[z] = total.astype(BF16)


def separator_kernel(parts, b_sep, dinv, x_sep, copies):
    for s2 in range(4):
        update = parts[0, s2].astype(F32)
        for z in range(1, 4):
            update = update + parts[z, s2].astype(F32)
        values = []
        for h in range(2):
            s = 2 * s2 + h
            reduced = b_sep[s].astype(F32) - update[8 * h : 8 * h + 8]
            forward_sep = lax.dot_general(
                reduced.astype(BF16), dinv[s], (((1,), (1,)), ((), ())), preferred_element_type=F32
            ).astype(BF16)
            value = jnp.dot(forward_sep, dinv[s], preferred_element_type=F32)
            x_sep[s] = value
            values.append(value)
        both = jnp.concatenate(values, axis=0).astype(BF16)
        for z in range(4):
            copies[z, s2] = both


def swap_core(values):
    return lax.ppermute(values, "core", [(0, 1), (1, 0)])


def exchange(values, axis):
    return lax.all_to_all(values, axis, 0, 0, tiled=True)


def shards(b_leaf, dinv_leaf, b_sep, dinv_sep, coupling, pattern):
    shape = jax.ShapeDtypeStruct
    same_core = lax.all_gather(b_leaf, "x", axis=0, tiled=False)
    core = lax.axis_index("core")
    other_core = swap_core(same_core)
    first = jnp.where(core == 0, same_core, other_core)
    second = jnp.where(core == 0, other_core, same_core)
    right = jnp.stack([first, second]).reshape(2, 4, 8, 4, 8, 256)
    right = jnp.transpose(right, (2, 0, 3, 1, 4, 5)).reshape(8, 256, 256)
    solved = jnp.einsum(
        "lrk,ljk->lrj", right, dinv_leaf, preferred_element_type=F32
    ).astype(BF16)
    sums = exchange(forward(pattern, solved, coupling), ("zl", "y"))
    sums = exchange(small(add_kernel, shape((4, 4, 16, 256), BF16), (sums,), "add_sums"), "zh")
    x_sep, copies = small(
        separator_kernel,
        (shape((8, 8, 256), F32), shape((4, 4, 16, 256), BF16)),
        (sums, b_sep, dinv_sep),
        "solve_separators",
    )
    values = exchange(copies, "zh")
    values = exchange(jnp.broadcast_to(values[None], (8,) + values.shape), ("zl", "y"))
    kept, sent = backward(pattern, values, coupling)
    pair = kept + swap_core(sent).astype(F32)
    total = jnp.sum(exchange(pair.astype(BF16), "x").astype(F32), axis=0)
    solved_share = jnp.einsum(
        "lrk,ljk->lrj", b_leaf, dinv_leaf, preferred_element_type=F32
    ).astype(BF16)
    corrected = (solved_share.astype(F32) - total).astype(BF16)
    x_leaf = jnp.einsum("lrk,lkj->lrj", corrected, dinv_leaf, preferred_element_type=F32)
    return (x_leaf, x_sep)


def solution(mesh):
    prow, pcol = ("x", "core"), ("zh", "zl", "y")
    chips = Mesh(mesh.devices.reshape(4, 2, 4, 2, 4), prow + pcol)
    return jax.shard_map(
        shards,
        mesh=chips,
        in_specs=(
            P(pcol, prow, None),
            P(pcol, None, None),
            P(prow, pcol, None),
            P(prow, None, None),
            P(prow, pcol, None, None),
            P(prow, pcol),
        ),
        out_specs=(P(pcol, prow, None), P(prow, pcol, None)),
        check_vma=False,
    )
```

```python
import jax
import jax.numpy as jnp
from jax import lax
from jax.experimental import pallas as pl
from jax.experimental.pallas import tpu as pltpu
from jax.sharding import Mesh, PartitionSpec as P

BF16 = jnp.bfloat16
F32 = jnp.float32
SMEM = pl.BlockSpec(memory_space=pltpu.SMEM)
VMEM = pl.BlockSpec(memory_space=pltpu.VMEM)


def forward_kernel(pattern, solved, coupling, out):
    for s2 in range(4):
        halves = []
        for s in (2 * s2, 2 * s2 + 1):
            total = None
            for l in range(8):
                left = solved[l] * pattern[s, l].astype(F32).astype(BF16)
                term = lax.dot_general(
                    left, coupling[s, l], (((1,), (1,)), ((), ())), preferred_element_type=F32
                )
                total = term if total is None else total + term
            halves.append(total.reshape(8, 4, 8, 256))
        out[:, :, s2] = jnp.concatenate(halves, axis=2).astype(BF16)


def forward(pattern, solved, coupling):
    return pl.pallas_call(
        forward_kernel,
        out_shape=jax.ShapeDtypeStruct((8, 4, 4, 16, 256), BF16),
        in_specs=[SMEM, VMEM, VMEM],
        out_specs=VMEM,
        compiler_params=pltpu.CompilerParams(vmem_limit_bytes=16 << 20),
        cost_estimate=pl.CostEstimate(flops=2 << 30, bytes_accessed=11 << 20, transcendentals=0),
        name="forward_sums",
    )(pattern, solved, coupling)


def backward_kernel(pattern, values, coupling, kept, sent, left):
    core, zh = lax.axis_index("core"), lax.axis_index("zh")
    for s2 in range(4):
        both = values[:, :, s2].astype(F32)
        for h in range(2):
            rows = both[:, :, 8 * h : 8 * h + 8].reshape(256, 256)
            left[2 * s2 + h] = rows.astype(BF16)
    for l in range(8):
        total = None
        for s in range(8):
            rows = left[s] * pattern[s, l].astype(F32).astype(BF16)
            term = jnp.dot(rows, coupling[s, l], preferred_element_type=F32)
            total = term if total is None else total + term
        parts = total.reshape(2, 4, 4, 8, 256)
        for y in range(0, 4, 2):
            both = jnp.concatenate([parts[:, y], parts[:, y + 1]], axis=2)
            mine = jnp.where(core == 0, both[0], both[1])
            others = jnp.where(core == 0, both[1], both[0]).astype(BF16)
            for d in range(4):
                x = lax.rem(zh + d, 4)
                kept[x, l, 8 * y : 8 * y + 16] = mine[d]
                sent[x, l, 8 * y : 8 * y + 16] = others[d]


def backward(pattern, values, coupling):
    def piece(kind):
        return jax.ShapeDtypeStruct((4, 8, 32, 256), kind)

    return pl.pallas_call(
        backward_kernel,
        out_shape=(piece(F32), piece(BF16)),
        in_specs=[SMEM, VMEM, VMEM],
        out_specs=(VMEM,) * 2,
        scratch_shapes=[
            pltpu.VMEM((8, 256, 256), BF16),
        ],
        compiler_params=pltpu.CompilerParams(vmem_limit_bytes=16 << 20),
        cost_estimate=pl.CostEstimate(flops=2 << 30, bytes_accessed=11 << 20, transcendentals=0),
        name="backward_sums",
    )(pattern, values, coupling)


def small(body, out_shape, inputs, name):
    return pl.pallas_call(
        body,
        out_shape=out_shape,
        in_specs=[VMEM] * len(inputs),
        out_specs=jax.tree.map(lambda _: VMEM, out_shape),
        compiler_params=pltpu.CompilerParams(vmem_limit_bytes=16 << 20),
        cost_estimate=pl.CostEstimate(flops=1 << 28, bytes_accessed=2 << 20, transcendentals=0),
        name=name,
    )(*inputs)


def add_kernel(parts, *outs):
    zh = lax.axis_index("zh")
    for d, out in enumerate(outs):
        z = lax.rem(zh + d, 4)
        total = parts[0, z].astype(F32)
        for source in range(1, 8):
            total = total + parts[source, z].astype(F32)
        out[...] = total.astype(out.dtype)


def separator_kernel(own, part1, part2, part3, b_sep, dinv, x_sep, x_send):
    for s2 in range(4):
        update = own[s2] + part1[s2].astype(F32) + part2[s2].astype(F32) + part3[s2].astype(F32)
        values = []
        for h in range(2):
            s = 2 * s2 + h
            reduced = b_sep[s].astype(F32) - update[8 * h : 8 * h + 8]
            forward_sep = lax.dot_general(
                reduced.astype(BF16), dinv[s], (((1,), (1,)), ((), ())), preferred_element_type=F32
            ).astype(BF16)
            value = jnp.dot(forward_sep, dinv[s], preferred_element_type=F32)
            x_sep[s] = value
            values.append(value)
        x_send[s2] = jnp.concatenate(values, axis=0).astype(BF16)


def spread_kernel(near0, near1, near2, near3, out):
    for copy in range(8):
        for d, near in enumerate((near0, near1, near2, near3)):
            out[copy, d] = near[...]


def swap_core(values):
    return lax.ppermute(values, "core", [(0, 1), (1, 0)])


def send_on(values, distance):
    return lax.ppermute(values, "zh", [(i, (i + distance) % 4) for i in range(4)])


def exchange(values, axis):
    return lax.all_to_all(values, axis, 0, 0, tiled=True)


def shards(b_leaf, dinv_leaf, b_sep, dinv_sep, coupling, pattern):
    shape = jax.ShapeDtypeStruct
    same_core = lax.all_gather(b_leaf, "x", axis=0, tiled=False)
    core = lax.axis_index("core")
    other_core = swap_core(same_core)
    first = jnp.where(core == 0, same_core, other_core)
    second = jnp.where(core == 0, other_core, same_core)
    right = jnp.stack([first, second]).reshape(2, 4, 8, 4, 8, 256)
    right = jnp.transpose(right, (2, 0, 3, 1, 4, 5)).reshape(8, 256, 256)
    solved = jnp.einsum(
        "lrk,ljk->lrj", right, dinv_leaf, preferred_element_type=F32
    ).astype(BF16)
    sums = exchange(forward(pattern, solved, coupling), ("zl", "y"))
    block = (4, 16, 256)
    own, *sums = small(
        add_kernel, (shape(block, F32),) + (shape(block, BF16),) * 3, (sums,), "add_sums"
    )
    sums = [send_on(part, d + 1) for d, part in enumerate(sums)]
    x_sep, x_send = small(
        separator_kernel,
        (shape((8, 8, 256), F32), shape(block, BF16)),
        (own, *sums, b_sep, dinv_sep),
        "solve_separators",
    )
    near = (x_send, send_on(x_send, 3), send_on(x_send, 2), send_on(x_send, 1))
    values = small(spread_kernel, shape((8, 4) + block, BF16), near, "copy_values")
    values = exchange(values, ("zl", "y"))
    kept, sent = backward(pattern, values, coupling)
    pair = kept + swap_core(sent).astype(F32)
    total = jnp.sum(exchange(pair.astype(BF16), "x").astype(F32), axis=0)
    solved_share = jnp.einsum(
        "lrk,ljk->lrj", b_leaf, dinv_leaf, preferred_element_type=F32
    ).astype(BF16)
    corrected = (solved_share.astype(F32) - total).astype(BF16)
    x_leaf = jnp.einsum("lrk,lkj->lrj", corrected, dinv_leaf, preferred_element_type=F32)
    return (x_leaf, x_sep)


def solution(mesh):
    prow, pcol = ("x", "core"), ("zh", "zl", "y")
    chips = Mesh(mesh.devices.reshape(4, 2, 4, 2, 4), prow + pcol)
    return jax.shard_map(
        shards,
        mesh=chips,
        in_specs=(
            P(pcol, prow, None),
            P(pcol, None, None),
            P(prow, pcol, None),
            P(prow, None, None),
            P(prow, pcol, None, None),
            P(prow, pcol),
        ),
        out_specs=(P(pcol, prow, None), P(prow, pcol, None)),
        check_vma=False,
    )
```

```python
import jax
import jax.numpy as jnp
from jax import lax
from jax.experimental import pallas as pl
from jax.experimental.pallas import tpu as pltpu
from jax.sharding import Mesh, PartitionSpec as P

BF16 = jnp.bfloat16
F32 = jnp.float32
SMEM = pl.BlockSpec(memory_space=pltpu.SMEM)
VMEM = pl.BlockSpec(memory_space=pltpu.VMEM)


def forward_kernel(pattern, solved, coupling, out):
    for s2 in range(4):
        halves = []
        for s in (2 * s2, 2 * s2 + 1):
            total = None
            for l in range(8):
                left = solved[l] * pattern[s, l].astype(F32).astype(BF16)
                term = lax.dot_general(
                    left, coupling[s, l], (((1,), (1,)), ((), ())), preferred_element_type=F32
                )
                total = term if total is None else total + term
            halves.append(total.reshape(8, 4, 8, 256))
        out[:, :, s2] = jnp.concatenate(halves, axis=2).astype(BF16)


def forward(pattern, solved, coupling):
    return pl.pallas_call(
        forward_kernel,
        out_shape=jax.ShapeDtypeStruct((8, 4, 4, 16, 256), BF16),
        in_specs=[SMEM, VMEM, VMEM],
        out_specs=VMEM,
        compiler_params=pltpu.CompilerParams(vmem_limit_bytes=16 << 20),
        cost_estimate=pl.CostEstimate(flops=2 << 30, bytes_accessed=11 << 20, transcendentals=0),
        name="forward_sums",
    )(pattern, solved, coupling)


def backward_kernel(pattern, values, coupling, kept, sent, left):
    core = lax.axis_index("core")
    for s2 in range(4):
        both = values[:, :, s2].astype(F32)
        for h in range(2):
            rows = both[:, :, 8 * h : 8 * h + 8].reshape(256, 256)
            left[2 * s2 + h] = rows.astype(BF16)
    for l in range(8):
        total = None
        for s in range(8):
            rows = left[s] * pattern[s, l].astype(F32).astype(BF16)
            term = jnp.dot(rows, coupling[s, l], preferred_element_type=F32)
            total = term if total is None else total + term
        parts = total.reshape(2, 4, 4, 8, 256)
        for y in range(0, 4, 2):
            both = jnp.concatenate([parts[:, y], parts[:, y + 1]], axis=2)
            kept[:, l, 8 * y : 8 * y + 16] = jnp.where(core == 0, both[0], both[1])
            sent[:, l, 8 * y : 8 * y + 16] = jnp.where(core == 0, both[1], both[0]).astype(BF16)


def backward(pattern, values, coupling):
    def piece(kind):
        return jax.ShapeDtypeStruct((4, 8, 32, 256), kind)

    return pl.pallas_call(
        backward_kernel,
        out_shape=(piece(F32), piece(BF16)),
        in_specs=[SMEM, VMEM, VMEM],
        out_specs=(VMEM,) * 2,
        scratch_shapes=[
            pltpu.VMEM((8, 256, 256), BF16),
        ],
        compiler_params=pltpu.CompilerParams(vmem_limit_bytes=16 << 20),
        cost_estimate=pl.CostEstimate(flops=2 << 30, bytes_accessed=11 << 20, transcendentals=0),
        name="backward_sums",
    )(pattern, values, coupling)


def small(body, out_shape, inputs, name, scratch=()):
    return pl.pallas_call(
        body,
        out_shape=out_shape,
        in_specs=[VMEM] * len(inputs),
        out_specs=jax.tree.map(lambda _: VMEM, out_shape),
        scratch_shapes=scratch,
        compiler_params=pltpu.CompilerParams(vmem_limit_bytes=16 << 20),
        cost_estimate=pl.CostEstimate(flops=1 << 28, bytes_accessed=2 << 20, transcendentals=0),
        name=name,
    )(*inputs)


def add_kernel(parts, b_sep, out):
    zh = lax.axis_index("zh")
    own = b_sep[...].astype(F32).reshape(4, 16, 256)
    for z in range(4):
        total = parts[0, z].astype(F32)
        for source in range(1, 8):
            total = total + parts[source, z].astype(F32)
        total = jnp.where(zh == z, own - total, -total).astype(BF16)
        for copy in range(4):
            out[copy, z] = total


def separator_kernel(parts, dinv, x_sep, copies, values):
    for s2 in range(4):
        reduced = parts[0, :, s2].astype(F32)
        for source in range(1, 4):
            reduced = reduced + parts[source, :, s2].astype(F32)
        halves = []
        for h in range(2):
            s = 2 * s2 + h
            rows = reduced[:, 8 * h : 8 * h + 8].reshape(32, 256).astype(BF16)
            forward_sep = lax.dot_general(
                rows, dinv[s], (((1,), (1,)), ((), ())), preferred_element_type=F32
            ).astype(BF16)
            value = jnp.dot(forward_sep, dinv[s], preferred_element_type=F32).reshape(4, 8, 256)
            values[:, s] = value
            halves.append(value)
        both = jnp.concatenate(halves, axis=1).astype(BF16)
        for copy in range(8):
            copies[copy, :, s2] = both
    x_sep[...] = values[lax.axis_index("zh")]


def swap_core(values):
    return lax.ppermute(values, "core", [(0, 1), (1, 0)])


def exchange(values, axis):
    return lax.all_to_all(values, axis, 0, 0, tiled=True)


def shards(b_leaf, dinv_leaf, b_sep, dinv_sep, coupling, pattern):
    shape = jax.ShapeDtypeStruct
    same_core = lax.all_gather(b_leaf, "x", axis=0, tiled=False)
    core = lax.axis_index("core")
    other_core = swap_core(same_core)
    first = jnp.where(core == 0, same_core, other_core)
    second = jnp.where(core == 0, other_core, same_core)
    right = jnp.stack([first, second]).reshape(2, 4, 8, 4, 8, 256)
    right = jnp.transpose(right, (2, 0, 3, 1, 4, 5)).reshape(8, 256, 256)
    solved = jnp.einsum(
        "lrk,ljk->lrj", right, dinv_leaf, preferred_element_type=F32
    ).astype(BF16)
    sums = exchange(forward(pattern, solved, coupling), ("zl", "y"))
    block = (4, 16, 256)
    sums = small(add_kernel, shape((4, 4) + block, BF16), (sums, b_sep), "add_sums")
    x_sep, copies = small(
        separator_kernel,
        (shape((8, 8, 256), F32), shape((8, 4) + block, BF16)),
        (exchange(sums, "zh"), dinv_sep),
        "solve_separators",
        [pltpu.VMEM((4, 8, 8, 256), F32)],
    )
    values = exchange(copies, ("zl", "y"))
    kept, sent = backward(pattern, values, coupling)
    pair = kept + swap_core(sent).astype(F32)
    total = jnp.sum(exchange(pair.astype(BF16), "x").astype(F32), axis=0)
    solved_share = jnp.einsum(
        "lrk,ljk->lrj", b_leaf, dinv_leaf, preferred_element_type=F32
    ).astype(BF16)
    corrected = (solved_share.astype(F32) - total).astype(BF16)
    x_leaf = jnp.einsum("lrk,lkj->lrj", corrected, dinv_leaf, preferred_element_type=F32)
    return (x_leaf, x_sep)


def solution(mesh):
    prow, pcol = ("x", "core"), ("zh", "zl", "y")
    chips = Mesh(mesh.devices.reshape(4, 2, 4, 2, 4), prow + pcol)
    return jax.shard_map(
        shards,
        mesh=chips,
        in_specs=(
            P(pcol, prow, None),
            P(pcol, None, None),
            P(prow, pcol, None),
            P(prow, None, None),
            P(prow, pcol, None, None),
            P(prow, pcol),
        ),
        out_specs=(P(pcol, prow, None), P(prow, pcol, None)),
        check_vma=False,
    )
```

```python
import jax
import jax.numpy as jnp
from jax import lax
from jax.experimental import pallas as pl
from jax.experimental.pallas import tpu as pltpu
from jax.sharding import Mesh, PartitionSpec as P

BF16 = jnp.bfloat16
F32 = jnp.float32
SMEM = pl.BlockSpec(memory_space=pltpu.SMEM)
VMEM = pl.BlockSpec(memory_space=pltpu.VMEM)


def forward_kernel(pattern, solved, coupling, out):
    x = lax.axis_index("x")
    for s2 in range(4):
        halves = []
        for s in (2 * s2, 2 * s2 + 1):
            total = None
            for l in range(8):
                left = solved[l] * pattern[s, l].astype(F32).astype(BF16)
                term = lax.dot_general(
                    left, coupling[s, l], (((1,), (1,)), ((), ())), preferred_element_type=F32
                )
                total = term if total is None else total + term
            halves.append(total.reshape(2, 4, 4, 8, 256))
        both = jnp.concatenate(halves, axis=3).astype(BF16)
        for dx in range(4):
            out[:, :, lax.rem(x + dx, 4), s2] = both[:, :, dx]


def forward(pattern, solved, coupling):
    return pl.pallas_call(
        forward_kernel,
        out_shape=jax.ShapeDtypeStruct((2, 4, 4, 4, 16, 256), BF16),
        in_specs=[SMEM, VMEM, VMEM],
        out_specs=VMEM,
        compiler_params=pltpu.CompilerParams(vmem_limit_bytes=16 << 20),
        cost_estimate=pl.CostEstimate(flops=2 << 30, bytes_accessed=11 << 20, transcendentals=0),
        name="forward_sums",
    )(pattern, solved, coupling)


def backward_kernel(pattern, values, coupling, kept, sent, left):
    core = lax.axis_index("core")
    offset = lax.axis_index("zh") - lax.axis_index("x") + 4
    for s2 in range(4):
        both = values[:, :, s2].astype(F32)
        for h in range(2):
            rows = both[:, :, 8 * h : 8 * h + 8].reshape(256, 256)
            left[2 * s2 + h] = rows.astype(BF16)
    for l in range(8):
        total = None
        for s in range(8):
            rows = left[s] * pattern[s, l].astype(F32).astype(BF16)
            term = jnp.dot(rows, coupling[s, l], preferred_element_type=F32)
            total = term if total is None else total + term
        parts = total.reshape(2, 4, 4, 8, 256)
        for y in range(0, 4, 2):
            both = jnp.concatenate([parts[:, y], parts[:, y + 1]], axis=2)
            mine = jnp.where(core == 0, both[0], both[1])
            others = jnp.where(core == 0, both[1], both[0]).astype(BF16)
            for d in range(4):
                dx = lax.rem(offset + d, 4)
                kept[dx, l, 8 * y : 8 * y + 16] = mine[d]
                sent[dx, l, 8 * y : 8 * y + 16] = others[d]


def backward(pattern, values, coupling):
    def piece(kind):
        return jax.ShapeDtypeStruct((4, 8, 32, 256), kind)

    return pl.pallas_call(
        backward_kernel,
        out_shape=(piece(F32), piece(BF16)),
        in_specs=[SMEM, VMEM, VMEM],
        out_specs=(VMEM,) * 2,
        scratch_shapes=[
            pltpu.VMEM((8, 256, 256), BF16),
        ],
        compiler_params=pltpu.CompilerParams(vmem_limit_bytes=16 << 20),
        cost_estimate=pl.CostEstimate(flops=2 << 30, bytes_accessed=11 << 20, transcendentals=0),
        name="backward_sums",
    )(pattern, values, coupling)


def small(body, out_shape, inputs, name):
    return pl.pallas_call(
        body,
        out_shape=out_shape,
        in_specs=[VMEM] * len(inputs),
        out_specs=jax.tree.map(lambda _: VMEM, out_shape),
        compiler_params=pltpu.CompilerParams(vmem_limit_bytes=16 << 20),
        cost_estimate=pl.CostEstimate(flops=1 << 28, bytes_accessed=2 << 20, transcendentals=0),
        name=name,
    )(*inputs)


def add_kernel(parts, *outs):
    zh = lax.axis_index("zh")
    for d, out in enumerate(outs):
        z = lax.rem(zh + d, 4)
        total = parts[0, z].astype(F32)
        for source in range(1, 8):
            total = total + parts[source, z].astype(F32)
        out[...] = total.astype(out.dtype)


def separator_kernel(own, part1, part2, part3, b_sep, dinv, x_sep, x_send):
    for s2 in range(4):
        update = own[s2] + part1[s2].astype(F32) + part2[s2].astype(F32) + part3[s2].astype(F32)
        values = []
        for h in range(2):
            s = 2 * s2 + h
            reduced = b_sep[s].astype(F32) - update[8 * h : 8 * h + 8]
            forward_sep = lax.dot_general(
                reduced.astype(BF16), dinv[s], (((1,), (1,)), ((), ())), preferred_element_type=F32
            ).astype(BF16)
            value = jnp.dot(forward_sep, dinv[s], preferred_element_type=F32)
            x_sep[s] = value
            values.append(value)
        x_send[s2] = jnp.concatenate(values, axis=0).astype(BF16)


def spread_kernel(near0, near1, near2, near3, out):
    for copy in range(8):
        for d, near in enumerate((near0, near1, near2, near3)):
            out[copy, d] = near[...]


def swap_core(values):
    return lax.ppermute(values, "core", [(0, 1), (1, 0)])


def send_on(values, distance, axis):
    return lax.ppermute(values, axis, [(i, (i + distance) % 4) for i in range(4)])


def exchange(values, axis):
    return lax.all_to_all(values, axis, 0, 0, tiled=True)


def shards(b_leaf, dinv_leaf, b_sep, dinv_sep, coupling, pattern):
    shape = jax.ShapeDtypeStruct
    core = lax.axis_index("core")
    far, up, down = send_on(b_leaf, 2, "x"), send_on(b_leaf, 3, "x"), send_on(b_leaf, 1, "x")
    same_core = jnp.stack([b_leaf, up, far, down])
    other_core = swap_core(same_core)
    first = jnp.where(core == 0, same_core, other_core)
    second = jnp.where(core == 0, other_core, same_core)
    right = jnp.stack([first, second]).reshape(2, 4, 8, 4, 8, 256)
    right = jnp.transpose(right, (2, 0, 3, 1, 4, 5)).reshape(8, 256, 256)
    solved = jnp.einsum(
        "lrk,ljk->lrj", right, dinv_leaf, preferred_element_type=F32
    ).astype(BF16)
    block = (4, 16, 256)
    sums = forward(pattern, solved, coupling).reshape((8, 4) + block)
    sums = exchange(sums, ("zl", "y"))
    own, *sums = small(
        add_kernel, (shape(block, F32),) + (shape(block, BF16),) * 3, (sums,), "add_sums"
    )
    sums = [send_on(part, d + 1, "zh") for d, part in enumerate(sums)]
    x_sep, x_send = small(
        separator_kernel,
        (shape((8, 8, 256), F32), shape(block, BF16)),
        (own, *sums, b_sep, dinv_sep),
        "solve_separators",
    )
    near = (x_send, send_on(x_send, 3, "zh"), send_on(x_send, 2, "zh"), send_on(x_send, 1, "zh"))
    values = small(spread_kernel, shape((8, 4) + block, BF16), near, "copy_values")
    values = exchange(values, ("zl", "y"))
    kept, sent = backward(pattern, values, coupling)
    pair = kept + swap_core(sent).astype(F32)
    parts = [send_on(pair[dx].astype(BF16), dx, "x") for dx in (2, 1, 3)]
    total = pair[0] + sum(part.astype(F32) for part in parts)
    solved_share = jnp.einsum(
        "lrk,ljk->lrj", b_leaf, dinv_leaf, preferred_element_type=F32
    ).astype(BF16)
    corrected = (solved_share.astype(F32) - total).astype(BF16)
    x_leaf = jnp.einsum("lrk,lkj->lrj", corrected, dinv_leaf, preferred_element_type=F32)
    return (x_leaf, x_sep)


def solution(mesh):
    prow, pcol = ("x", "core"), ("zh", "zl", "y")
    chips = Mesh(mesh.devices.reshape(4, 2, 4, 2, 4), prow + pcol)
    return jax.shard_map(
        shards,
        mesh=chips,
        in_specs=(
            P(pcol, prow, None),
            P(pcol, None, None),
            P(prow, pcol, None),
            P(prow, None, None),
            P(prow, pcol, None, None),
            P(prow, pcol),
        ),
        out_specs=(P(pcol, prow, None), P(prow, pcol, None)),
        check_vma=False,
    )
```

```python
import jax
import jax.numpy as jnp
from jax import lax
from jax.experimental import pallas as pl
from jax.experimental.pallas import tpu as pltpu
from jax.sharding import Mesh, PartitionSpec as P

BF16 = jnp.bfloat16
F32 = jnp.float32
SMEM = pl.BlockSpec(memory_space=pltpu.SMEM)
VMEM = pl.BlockSpec(memory_space=pltpu.VMEM)


def forward_kernel(pattern, solved, coupling, out):
    x = lax.axis_index("x")
    for s2 in range(4):
        halves = []
        for s in (2 * s2, 2 * s2 + 1):
            total = None
            for l in range(8):
                left = solved[l] * pattern[s, l].astype(F32).astype(BF16)
                term = lax.dot_general(
                    left, coupling[s, l], (((1,), (1,)), ((), ())), preferred_element_type=F32
                )
                total = term if total is None else total + term
            halves.append(total.reshape(2, 4, 4, 8, 256))
        both = jnp.concatenate(halves, axis=3).astype(BF16)
        for dx in range(4):
            out[:, :, lax.rem(x + dx, 4), s2] = both[:, :, dx]


def forward(pattern, solved, coupling):
    return pl.pallas_call(
        forward_kernel,
        out_shape=jax.ShapeDtypeStruct((2, 4, 4, 4, 16, 256), BF16),
        in_specs=[SMEM, VMEM, VMEM],
        out_specs=VMEM,
        compiler_params=pltpu.CompilerParams(vmem_limit_bytes=16 << 20),
        cost_estimate=pl.CostEstimate(flops=2 << 30, bytes_accessed=11 << 20, transcendentals=0),
        name="forward_sums",
    )(pattern, solved, coupling)


def backward_kernel(pattern, values, coupling, kept, sent, left):
    core = lax.axis_index("core")
    offset = lax.axis_index("zh") - lax.axis_index("x") + 4
    for s2 in range(4):
        both = values[:, :, s2].astype(F32)
        for h in range(2):
            rows = both[:, :, 8 * h : 8 * h + 8].reshape(256, 256)
            left[2 * s2 + h] = rows.astype(BF16)
    for l in range(8):
        total = None
        for s in range(8):
            rows = left[s] * pattern[s, l].astype(F32).astype(BF16)
            term = jnp.dot(rows, coupling[s, l], preferred_element_type=F32)
            total = term if total is None else total + term
        parts = total.reshape(2, 4, 4, 8, 256)
        for y in range(0, 4, 2):
            both = jnp.concatenate([parts[:, y], parts[:, y + 1]], axis=2)
            mine = jnp.where(core == 0, both[0], both[1])
            others = jnp.where(core == 0, both[1], both[0]).astype(BF16)
            for d in range(4):
                dx = lax.rem(offset + d, 4)
                kept[dx, l, 8 * y : 8 * y + 16] = mine[d]
                sent[dx, l, 8 * y : 8 * y + 16] = others[d]


def backward(pattern, values, coupling):
    def piece(kind):
        return jax.ShapeDtypeStruct((4, 8, 32, 256), kind)

    return pl.pallas_call(
        backward_kernel,
        out_shape=(piece(F32), piece(BF16)),
        in_specs=[SMEM, VMEM, VMEM],
        out_specs=(VMEM,) * 2,
        scratch_shapes=[
            pltpu.VMEM((8, 256, 256), BF16),
        ],
        compiler_params=pltpu.CompilerParams(vmem_limit_bytes=16 << 20),
        cost_estimate=pl.CostEstimate(flops=2 << 30, bytes_accessed=11 << 20, transcendentals=0),
        name="backward_sums",
    )(pattern, values, coupling)


def small(body, out_shape, inputs, name):
    return pl.pallas_call(
        body,
        out_shape=out_shape,
        in_specs=[VMEM] * len(inputs),
        out_specs=jax.tree.map(lambda _: VMEM, out_shape),
        compiler_params=pltpu.CompilerParams(vmem_limit_bytes=16 << 20),
        cost_estimate=pl.CostEstimate(flops=1 << 28, bytes_accessed=2 << 20, transcendentals=0),
        name=name,
    )(*inputs)


def add_kernel(parts, *outs):
    zh = lax.axis_index("zh")
    for d, out in enumerate(outs):
        z = lax.rem(zh + d, 4)
        total = parts[0, z].astype(F32)
        for source in range(1, 8):
            total = total + parts[source, z].astype(F32)
        out[...] = total.astype(out.dtype)


def stack_kernel(piece0, piece1, piece2, piece3, out):
    for d, piece in enumerate((piece0, piece1, piece2, piece3)):
        out[d] = piece[...]


def separator_kernel(own, part1, part2, part3, b_sep, dinv, x_sep, x_send):
    for s2 in range(4):
        update = own[s2] + part1[s2].astype(F32) + part2[s2].astype(F32) + part3[s2].astype(F32)
        values = []
        for h in range(2):
            s = 2 * s2 + h
            reduced = b_sep[s].astype(F32) - update[8 * h : 8 * h + 8]
            forward_sep = lax.dot_general(
                reduced.astype(BF16), dinv[s], (((1,), (1,)), ((), ())), preferred_element_type=F32
            ).astype(BF16)
            value = jnp.dot(forward_sep, dinv[s], preferred_element_type=F32)
            x_sep[s] = value
            values.append(value)
        x_send[s2] = jnp.concatenate(values, axis=0).astype(BF16)


def copy_kernel(values, out):
    out[...] = values[...]


def spread_kernel(near0, near1, near2, near3, out):
    for copy in range(8):
        for d, near in enumerate((near0, near1, near2, near3)):
            out[copy, d] = near[...]


def swap_core(values):
    return lax.ppermute(values, "core", [(0, 1), (1, 0)])


def send_on(values, distance, axis):
    return lax.ppermute(values, axis, [(i, (i + distance) % 4) for i in range(4)])


def exchange(values, axis):
    return lax.all_to_all(values, axis, 0, 0, tiled=True)


def shards(b_leaf, dinv_leaf, b_sep, dinv_sep, coupling, pattern):
    shape = jax.ShapeDtypeStruct
    core = lax.axis_index("core")
    far, up, down = send_on(b_leaf, 2, "x"), send_on(b_leaf, 3, "x"), send_on(b_leaf, 1, "x")
    same_core = small(
        stack_kernel, shape((4, 8, 32, 256), BF16), (b_leaf, up, far, down), "stack_blocks"
    )
    other_core = swap_core(same_core)
    first = jnp.where(core == 0, same_core, other_core)
    second = jnp.where(core == 0, other_core, same_core)
    right = jnp.stack([first, second]).reshape(2, 4, 8, 4, 8, 256)
    right = jnp.transpose(right, (2, 0, 3, 1, 4, 5)).reshape(8, 256, 256)
    solved = jnp.einsum(
        "lrk,ljk->lrj", right, dinv_leaf, preferred_element_type=F32
    ).astype(BF16)
    block = (4, 16, 256)
    sums = forward(pattern, solved, coupling).reshape((8, 4) + block)
    sums = exchange(sums, ("zl", "y"))
    own, *sums = small(
        add_kernel, (shape(block, F32),) + (shape(block, BF16),) * 3, (sums,), "add_sums"
    )
    sums = [send_on(part, d + 1, "zh") for d, part in enumerate(sums)]
    solution_sep, x_send = small(
        separator_kernel,
        (shape((8, 8, 256), F32), shape(block, BF16)),
        (own, *sums, b_sep, dinv_sep),
        "solve_separators",
    )
    x_sep = small(copy_kernel, shape((8, 8, 256), F32), (solution_sep,), "copy_solution")
    near = (x_send, send_on(x_send, 3, "zh"), send_on(x_send, 2, "zh"), send_on(x_send, 1, "zh"))
    values = small(spread_kernel, shape((8, 4) + block, BF16), near, "copy_values")
    values = exchange(values, ("zl", "y"))
    kept, sent = backward(pattern, values, coupling)
    pair = kept + swap_core(sent).astype(F32)
    parts = [send_on(pair[dx].astype(BF16), dx, "x") for dx in (2, 1, 3)]
    total = pair[0] + sum(part.astype(F32) for part in parts)
    solved_share = jnp.einsum(
        "lrk,ljk->lrj", b_leaf, dinv_leaf, preferred_element_type=F32
    ).astype(BF16)
    corrected = (solved_share.astype(F32) - total).astype(BF16)
    x_leaf = jnp.einsum("lrk,lkj->lrj", corrected, dinv_leaf, preferred_element_type=F32)
    return (x_leaf, x_sep)


def solution(mesh):
    prow, pcol = ("x", "core"), ("zh", "zl", "y")
    chips = Mesh(mesh.devices.reshape(4, 2, 4, 2, 4), prow + pcol)
    return jax.shard_map(
        shards,
        mesh=chips,
        in_specs=(
            P(pcol, prow, None),
            P(pcol, None, None),
            P(prow, pcol, None),
            P(prow, None, None),
            P(prow, pcol, None, None),
            P(prow, pcol),
        ),
        out_specs=(P(pcol, prow, None), P(prow, pcol, None)),
        check_vma=False,
    )
```

```python
import jax
import jax.numpy as jnp
from jax import lax
from jax.experimental import pallas as pl
from jax.experimental.pallas import tpu as pltpu
from jax.sharding import Mesh, PartitionSpec as P

BF16 = jnp.bfloat16
F32 = jnp.float32
SMEM = pl.BlockSpec(memory_space=pltpu.SMEM)
VMEM = pl.BlockSpec(memory_space=pltpu.VMEM)


def forward_kernel(pattern, solved, coupling, out):
    x = lax.axis_index("x")
    for s2 in range(4):
        halves = []
        for s in (2 * s2, 2 * s2 + 1):
            total = None
            for l in range(8):
                left = solved[l] * pattern[s, l].astype(F32).astype(BF16)
                term = lax.dot_general(
                    left, coupling[s, l], (((1,), (1,)), ((), ())), preferred_element_type=F32
                )
                total = term if total is None else total + term
            halves.append(total.reshape(2, 4, 4, 8, 256))
        both = jnp.concatenate(halves, axis=3).astype(BF16)
        for dx in range(4):
            out[:, :, lax.rem(x + dx, 4), s2] = both[:, :, dx]


def forward(pattern, solved, coupling):
    return pl.pallas_call(
        forward_kernel,
        out_shape=jax.ShapeDtypeStruct((2, 4, 4, 4, 16, 256), BF16),
        in_specs=[SMEM, VMEM, VMEM],
        out_specs=VMEM,
        compiler_params=pltpu.CompilerParams(vmem_limit_bytes=16 << 20),
        cost_estimate=pl.CostEstimate(flops=2 << 30, bytes_accessed=11 << 20, transcendentals=0),
        name="forward_sums",
    )(pattern, solved, coupling)


def backward_kernel(pattern, values, coupling, kept, sent, left):
    core = lax.axis_index("core")
    offset = lax.axis_index("zh") - lax.axis_index("x") + 4
    for s2 in range(4):
        both = values[:, :, s2].astype(F32)
        for h in range(2):
            rows = both[:, :, 8 * h : 8 * h + 8].reshape(256, 256)
            left[2 * s2 + h] = rows.astype(BF16)
    for l in range(8):
        total = None
        for s in range(8):
            rows = left[s] * pattern[s, l].astype(F32).astype(BF16)
            term = jnp.dot(rows, coupling[s, l], preferred_element_type=F32)
            total = term if total is None else total + term
        parts = total.reshape(2, 4, 4, 8, 256)
        for y in range(0, 4, 2):
            both = jnp.concatenate([parts[:, y], parts[:, y + 1]], axis=2)
            mine = jnp.where(core == 0, both[0], both[1])
            others = jnp.where(core == 0, both[1], both[0]).astype(BF16)
            for d in range(4):
                dx = lax.rem(offset + d, 4)
                kept[dx, l, 8 * y : 8 * y + 16] = mine[d]
                sent[dx, l, 8 * y : 8 * y + 16] = others[d]


def backward(pattern, values, coupling):
    def piece(kind):
        return jax.ShapeDtypeStruct((4, 8, 32, 256), kind)

    return pl.pallas_call(
        backward_kernel,
        out_shape=(piece(F32), piece(BF16)),
        in_specs=[SMEM, VMEM, VMEM],
        out_specs=(VMEM,) * 2,
        scratch_shapes=[
            pltpu.VMEM((8, 256, 256), BF16),
        ],
        compiler_params=pltpu.CompilerParams(vmem_limit_bytes=16 << 20),
        cost_estimate=pl.CostEstimate(flops=2 << 30, bytes_accessed=11 << 20, transcendentals=0),
        name="backward_sums",
    )(pattern, values, coupling)


def small(body, out_shape, inputs, name):
    return pl.pallas_call(
        body,
        out_shape=out_shape,
        in_specs=[VMEM] * len(inputs),
        out_specs=jax.tree.map(lambda _: VMEM, out_shape),
        compiler_params=pltpu.CompilerParams(vmem_limit_bytes=16 << 20),
        cost_estimate=pl.CostEstimate(flops=1 << 28, bytes_accessed=2 << 20, transcendentals=0),
        name=name,
    )(*inputs)


def add_kernel(parts, *outs):
    zh = lax.axis_index("zh")
    for d, out in enumerate(outs):
        z = lax.rem(zh + d, 4)
        total = parts[0, z].astype(F32)
        for source in range(1, 8):
            total = total + parts[source, z].astype(F32)
        out[...] = total.astype(out.dtype)


def stack_kernel(piece0, piece1, piece2, piece3, out):
    for d, piece in enumerate((piece0, piece1, piece2, piece3)):
        out[d] = piece[...]


def separator_kernel(own, part1, part2, part3, b_sep, dinv, x_sep, x_send):
    for s2 in range(4):
        update = own[s2] + part1[s2].astype(F32) + part2[s2].astype(F32) + part3[s2].astype(F32)
        values = []
        for h in range(2):
            s = 2 * s2 + h
            reduced = b_sep[s].astype(F32) - update[8 * h : 8 * h + 8]
            forward_sep = lax.dot_general(
                reduced.astype(BF16), dinv[s], (((1,), (1,)), ((), ())), preferred_element_type=F32
            ).astype(BF16)
            value = jnp.dot(forward_sep, dinv[s], preferred_element_type=F32)
            x_sep[s] = value
            values.append(value)
        x_send[s2] = jnp.concatenate(values, axis=0).astype(BF16)


def copy_kernel(values, out):
    out[...] = values[...]


def spread_kernel(near0, near1, near2, near3, out):
    for copy in range(8):
        for d, near in enumerate((near0, near1, near2, near3)):
            out[copy, d] = near[...]


def swap_core(values):
    return lax.ppermute(values, "core", [(0, 1), (1, 0)])


def send_on(values, distance, axis):
    return lax.ppermute(values, axis, [(i, (i + distance) % 4) for i in range(4)])


def exchange(values, axis):
    return lax.all_to_all(values, axis, 0, 0, tiled=True)


def shards(b_leaf, dinv_leaf, b_sep, dinv_sep, coupling, pattern):
    shape = jax.ShapeDtypeStruct
    core = lax.axis_index("core")
    far, up, down = send_on(b_leaf, 2, "x"), send_on(b_leaf, 3, "x"), send_on(b_leaf, 1, "x")
    own = small(copy_kernel, shape((8, 32, 256), BF16), (b_leaf,), "copy_own")
    same_core = small(
        stack_kernel, shape((4, 8, 32, 256), BF16), (own, up, far, down), "stack_blocks"
    )
    other_core = swap_core(same_core)
    first = jnp.where(core == 0, same_core, other_core)
    second = jnp.where(core == 0, other_core, same_core)
    right = jnp.stack([first, second]).reshape(2, 4, 8, 4, 8, 256)
    right = jnp.transpose(right, (2, 0, 3, 1, 4, 5)).reshape(8, 256, 256)
    solved = jnp.einsum(
        "lrk,ljk->lrj", right, dinv_leaf, preferred_element_type=F32
    ).astype(BF16)
    block = (4, 16, 256)
    sums = forward(pattern, solved, coupling).reshape((8, 4) + block)
    sums = exchange(sums, ("zl", "y"))
    own, *sums = small(
        add_kernel, (shape(block, F32),) + (shape(block, BF16),) * 3, (sums,), "add_sums"
    )
    sums = [send_on(part, d + 1, "zh") for d, part in enumerate(sums)]
    solution_sep, x_send = small(
        separator_kernel,
        (shape((8, 8, 256), F32), shape(block, BF16)),
        (own, *sums, b_sep, dinv_sep),
        "solve_separators",
    )
    x_sep = small(copy_kernel, shape((8, 8, 256), F32), (solution_sep,), "copy_solution")
    near = (x_send, send_on(x_send, 3, "zh"), send_on(x_send, 2, "zh"), send_on(x_send, 1, "zh"))
    values = small(spread_kernel, shape((8, 4) + block, BF16), near, "copy_values")
    values = exchange(values, ("zl", "y"))
    kept, sent = backward(pattern, values, coupling)
    pair = kept + swap_core(sent).astype(F32)
    parts = [send_on(pair[dx].astype(BF16), dx, "x") for dx in (2, 1, 3)]
    total = pair[0] + sum(part.astype(F32) for part in parts)
    solved_share = jnp.einsum(
        "lrk,ljk->lrj", b_leaf, dinv_leaf, preferred_element_type=F32
    ).astype(BF16)
    corrected = (solved_share.astype(F32) - total).astype(BF16)
    x_leaf = jnp.einsum("lrk,lkj->lrj", corrected, dinv_leaf, preferred_element_type=F32)
    return (x_leaf, x_sep)


def solution(mesh):
    prow, pcol = ("x", "core"), ("zh", "zl", "y")
    chips = Mesh(mesh.devices.reshape(4, 2, 4, 2, 4), prow + pcol)
    return jax.shard_map(
        shards,
        mesh=chips,
        in_specs=(
            P(pcol, prow, None),
            P(pcol, None, None),
            P(prow, pcol, None),
            P(prow, None, None),
            P(prow, pcol, None, None),
            P(prow, pcol),
        ),
        out_specs=(P(pcol, prow, None), P(prow, pcol, None)),
        check_vma=False,
    )
```
